512 devices in a mesh: pipe: 16 (over z_hi, y), expert: 32 (over x, z_lo, core).
Axes of the slice: x: 4, y: 4, z: 16 (z_hi: 4, z_lo: 4; z = z_hi * 4 + z_lo), core: 2. Of those that a mesh axis runs over, the one named last changes fastest.
Arguments:
- grad_out: bfloat16 [16, 4096, 3584], P('pipe', 'expert'), may hold values from -0.29882812 to 0.29882812
- expert_ids: int32 [16, 4096, 8], P('pipe', 'expert'), may hold values from 0 to 31, as said below
- slot_pos: int32 [16, 4096, 8], P('pipe', 'expert'), may hold values from -1 to 35, as said below
- gate_probs: float32 [16, 4096, 8], P('pipe', 'expert'), may hold values from 0.1 to 1
- saved_pre: bfloat16 [16, 32, 32, 36, 512], P('pipe', None, 'expert'), may hold values from -6 to 6
Outputs:
- expert_grad: bfloat16 [16, 32, 256, 3584], P('pipe', 'expert')
The draws below stay inside these ranges and needn't reach their ends.
Inputs may be any that keep to these rules, and one draw needn't show every extreme that they name: `expert_ids`: each row names 8 different experts. `slot_pos`: within the 128 rows of one device, the pairs naming one expert take positions 0, 1, 2 and so on in order of row and then choice, up to 35; later such pairs hold -1. In every such block some expert fills all 36 positions.
All inputs are finite; a program needn't handle non-finite values.
Results may differ from the reference program's by a relative error of at most 0.0065.
Values may be sent and summed in bfloat16 or wider, within the bound.
A program may use at most 128 MiB of HBM per device.

```python
import jax
import jax.numpy as jnp
from jax import lax

D = 3584
EXPERTS = 32
TOP = 8
TOK_DEV = 128
CAP = 36
SLAB = 256
TOK_E = 4096
N_PIPE = 16
N_EXPERT = 32


def routing_tables(key):
    k_perm, k_base, k_common, k_pick = jax.random.split(key, 4)
    blocks = N_PIPE * N_EXPERT
    order = jax.random.permutation(k_perm, EXPERTS).astype(jnp.int32)
    base = jax.random.randint(k_base, (blocks, TOK_DEV), 0, EXPERTS, dtype=jnp.int32)
    common = jax.random.randint(k_common, (), 0, EXPERTS, dtype=jnp.int32)
    ranks = jax.vmap(lambda sub: jax.random.permutation(sub, TOK_DEV))(jax.random.split(k_pick, blocks))
    base = jnp.where(ranks < CAP, common, base).astype(jnp.int32)
    stride = EXPERTS // TOP
    position = (base[:, :, None] + stride * jnp.arange(TOP, dtype=jnp.int32)[None, None, :]) % EXPERTS
    chosen = order[position].astype(jnp.int32)
    flat = chosen.reshape(blocks, TOK_DEV * TOP)
    onehot = (flat[:, :, None] == jnp.arange(EXPERTS, dtype=jnp.int32)[None, None, :]).astype(jnp.int32)
    seen = jnp.cumsum(onehot, axis=1) - onehot
    rank = jnp.sum(seen * onehot, axis=2)
    slots = jnp.where(rank < CAP, rank, -1).astype(jnp.int32)
    return (chosen.reshape(N_PIPE, N_EXPERT * TOK_DEV, TOP), slots.reshape(N_PIPE, N_EXPERT * TOK_DEV, TOP))


def draw_expert_ids(key, part):
    return routing_tables(key)[0]


def draw_slot_pos(key, part):
    return routing_tables(key)[1]


def level_of(rng, dims, cuts, least, top_value):
    def one(dim, shards_of):
        steps = jax.random.uniform(jax.random.fold_in(jax.random.fold_in(rng, 6), dim), (shards_of,), jnp.float32, least / len(cuts), top_value / len(cuts))
        return jnp.repeat(jnp.exp(steps), dims[dim] // shards_of).reshape((-1,) + (1,) * (len(dims) - dim - 1))

    factor_of = one(*cuts[0])
    for cut in cuts[1:]:
        factor_of = factor_of * one(*cut)
    return factor_of


def noise(rng, dims, spread, most, cuts=(), kind=jnp.bfloat16):
    result = spread * jax.random.normal(rng, dims, jnp.float32)
    if cuts:
        result = result * level_of(rng, dims, cuts, -0.22, 0.18)
    return jnp.clip(result, -most, most).astype(kind)


def setup_inputs(seed: int = 0) -> dict:
    key_of = jax.random.split(jax.random.key(seed), 6)
    grad_out = noise(key_of[0], (N_PIPE, TOK_E, D), 0.05, 0.29882812, ((0, 16), (1, 32)))
    expert_ids = draw_expert_ids(jax.random.fold_in(key_of[5], 71), 0)
    slot_pos = draw_slot_pos(jax.random.fold_in(key_of[5], 71), 0)
    gate_probs = jnp.clip(0.1 + 0.9 * jax.random.uniform(key_of[3], (N_PIPE, TOK_E, TOP), jnp.float32) ** level_of(key_of[3], (N_PIPE, TOK_E, TOP), ((0, 16), (1, 32)), -0.2, 0.2), 0.1, 1.0)
    saved_pre = noise(key_of[4], (N_PIPE, N_EXPERT, EXPERTS, CAP, 2 * SLAB), 1.0, 6.0, ((0, 16), (2, 32)))
    return {"grad_out": grad_out, "expert_ids": expert_ids, "slot_pos": slot_pos, "gate_probs": gate_probs, "saved_pre": saved_pre}


def one_rank(grad_rows, chosen, slots, weights, saved):
    rows = grad_rows.shape[0]
    source = (jnp.arange(rows, dtype=jnp.int32) // TOK_DEV).astype(jnp.int32)
    limit = N_EXPERT * EXPERTS * CAP
    target = (source[:, None] * EXPERTS + chosen) * CAP + slots
    target = jnp.where(slots >= 0, target, limit).astype(jnp.int32)
    scaled = (weights[:, :, None] * grad_rows[:, None, :].astype(jnp.float32)).astype(jnp.bfloat16)
    buffer = jnp.zeros((limit, D), jnp.bfloat16)
    buffer = buffer.at[target.reshape(-1)].set(scaled.reshape(-1, D), mode="drop")
    buffer = buffer.reshape(N_EXPERT, EXPERTS, CAP, D)
    gate_part = saved[..., :SLAB].astype(jnp.float32)
    up_part = saved[..., SLAB:].astype(jnp.float32)
    hidden = (jax.nn.silu(gate_part) * up_part).astype(jnp.bfloat16)
    product = jnp.einsum("sech,secd->ehd", hidden.astype(jnp.float32), buffer.astype(jnp.float32))
    return product.astype(jnp.bfloat16)


def reference(grad_out, expert_ids, slot_pos, gate_probs, saved_pre):
    own = lax.map(lambda group: one_rank(*group), (grad_out, expert_ids, slot_pos, gate_probs, saved_pre))
    total = own.astype(jnp.float32) + own[::-1].astype(jnp.float32)
    return total.astype(jnp.bfloat16)
```

```python
import functools

import jax
import jax.numpy as jnp
from jax import lax
from jax.experimental import pallas as pl
from jax.experimental.pallas import tpu as pltpu
from jax.sharding import PartitionSpec as P

MESH = pl.DeviceIdType.MESH
COLS = 128
RING = 4
LINE = 4
HALF = RING * LINE
RECV_LAG = 6


def kernel(
    chunks, capacity,
    table_ref, grad_ref, saved_ref, out_ref,
    rows, tables, pre, hidden, spread, own, back,
    z_send, z_recv, x_send, x_recv, s_send, s_recv, e_send, e_recv, load_sem, pre_sem, tab_sem,
):
    e = lax.axis_index("expert")
    p = lax.axis_index("pipe")
    core = lax.rem(e, 2)
    zl = lax.rem(lax.div(e, 2), LINE)
    x = lax.div(e, 2 * LINE)
    x_left = lax.rem(x + RING - 1, RING)
    x_right = lax.rem(x + 1, RING)
    x_far = lax.rem(x + 2, RING)
    lane = zl * 2 + core
    up = {"expert": e + 2}
    down = {"expert": e - 2}
    right = {"expert": x_right * 2 * LINE + lane}
    left = {"expert": x_left * 2 * LINE + lane}
    sibling = {"expert": e + 1 - 2 * core}
    mirror = {"pipe": lax.axis_size("pipe") - 1 - p}
    sources = tables.shape[0]
    width = spread.shape[0]
    TAB = chunks

    def put(src, dst, ssem, rsem, where):
        return pltpu.make_async_remote_copy(
            src_ref=src, dst_ref=dst, send_sem=ssem, recv_sem=rsem, device_id=where, device_id_type=MESH
        )

    def block(buf, zz):
        return buf.at[core * HALF + x * LINE + zz]

    def column(buf, xx, of, first=0, count=LINE):
        return buf.at[pl.ds(of * HALF + xx * LINE + first, count)]

    def load(j):
        return pltpu.make_async_copy(
            grad_ref.at[:, pl.ds(pl.multiple_of(j * COLS, COLS), COLS)],
            block(rows.at[j], zl),
            load_sem.at[j],
        )

    table_load = pltpu.make_async_copy(table_ref, block(tables, zl), tab_sem)
    pre_load = pltpu.make_async_copy(saved_ref, pre, pre_sem)
    table_load.start()

    @pl.loop(0, chunks)
    def _(j):
        load(j).start()

    pre_load.start()

    barrier = pltpu.get_barrier_semaphore()
    for where in (right, left, sibling, mirror):
        pl.semaphore_signal(barrier, inc=1, device_id=where, device_id_type=MESH)

    @pl.when(zl < LINE - 1)
    def _():
        pl.semaphore_signal(barrier, inc=1, device_id=up, device_id_type=MESH)

    @pl.when(zl > 0)
    def _():
        pl.semaphore_signal(barrier, inc=1, device_id=down, device_id_type=MESH)

    pl.semaphore_wait(barrier, 4 + jnp.minimum(zl, 1) + jnp.minimum(LINE - 1 - zl, 1))

    def go_up(buf, q, hop):
        mine = block(buf, zl - hop)
        return put(mine, mine, z_send.at[q, 0, hop], z_recv.at[q, 0, hop], up)

    def go_down(buf, q, hop):
        mine = block(buf, zl + hop)
        return put(mine, mine, z_send.at[q, 1, hop], z_recv.at[q, 1, hop], down)

    def go_right(buf, q, hop):
        mine = column(buf, x, core) if hop == 0 else column(buf, x_left, core, 0, LINE // 2)
        return put(mine, mine, x_send.at[q, 0, hop], x_recv.at[q, 0, hop], right)

    def go_left(buf, q, hop):
        mine = column(buf, x, core) if hop == 0 else column(buf, x_right, core, LINE // 2, LINE // 2)
        return put(mine, mine, x_send.at[q, 1, hop], x_recv.at[q, 1, hop], left)

    def go_across(buf, q, k):
        mine = column(buf, (x, x_left, x_right, x_far)[k], core)
        return put(mine, mine, s_send.at[q, k], s_recv.at[q, k], sibling)

    def await_up(buf, q, hop):
        got = block(buf, zl - hop)
        put(got, got, z_send.at[q, 0, hop - 1], z_recv.at[q, 0, hop - 1], up).wait_recv()

    def await_down(buf, q, hop):
        got = block(buf, zl + hop)
        put(got, got, z_send.at[q, 1, hop - 1], z_recv.at[q, 1, hop - 1], down).wait_recv()

    def await_right(buf, q, hop):
        got = column(buf, x_left, core) if hop == 0 else column(buf, x_far, core, 0, LINE // 2)
        put(got, got, x_send.at[q, 0, hop], x_recv.at[q, 0, hop], right).wait_recv()

    def await_left(buf, q, hop):
        got = column(buf, x_right, core) if hop == 0 else column(buf, x_far, core, LINE // 2, LINE // 2)
        put(got, got, x_send.at[q, 1, hop], x_recv.at[q, 1, hop], left).wait_recv()

    def await_across(buf, q, k):
        got = column(buf, (x, x_left, x_right, x_far)[k], 1 - core)
        put(got, got, s_send.at[q, k], s_recv.at[q, k], sibling).wait_recv()

    def stage0(buf, q):
        @pl.when(zl < LINE - 1)
        def _():
            go_up(buf, q, 0).start()

        @pl.when(zl > 0)
        def _():
            go_down(buf, q, 0).start()

    def along_line(buf, q, hop):
        @pl.when(zl >= hop)
        def _():
            await_up(buf, q, hop)
            if hop < LINE - 1:

                @pl.when(zl < LINE - 1)
                def _():
                    go_up(buf, q, hop).start()

        @pl.when(zl < LINE - hop)
        def _():
            await_down(buf, q, hop)
            if hop < LINE - 1:

                @pl.when(zl > 0)
                def _():
                    go_down(buf, q, hop).start()

    def stage3(buf, q):
        along_line(buf, q, 3)
        go_right(buf, q, 0).start()
        go_left(buf, q, 0).start()
        go_across(buf, q, 0).start()

    def stage4(buf, q):
        await_right(buf, q, 0)
        go_right(buf, q, 1).start()
        go_across(buf, q, 1).start()
        await_left(buf, q, 0)
        go_left(buf, q, 1).start()
        go_across(buf, q, 2).start()

    def stage5(buf, q):
        await_right(buf, q, 1)
        await_left(buf, q, 1)
        go_across(buf, q, 3).start()

    def stage6(buf, q):
        for k in range(4):
            await_across(buf, q, k)

    def sent(buf, q):
        for hop in range(LINE - 1):

            @pl.when((zl >= hop) & (zl < LINE - 1))
            def _():
                go_up(buf, q, hop).wait_send()

            @pl.when((zl < LINE - hop) & (zl > 0))
            def _():
                go_down(buf, q, hop).wait_send()

        for hop in range(2):
            go_right(buf, q, hop).wait_send()
            go_left(buf, q, hop).wait_send()
        for k in range(4):
            go_across(buf, q, k).wait_send()

    def exchange(j):
        return put(own.at[j], back.at[j], e_send.at[j], e_recv.at[j], mirror)

    def make_hidden(first, count):
        @pl.loop(first, first + count)
        def _(s):
            gate = pre[s, :, :width].astype(jnp.float32)
            lift = pre[s, :, width:].astype(jnp.float32)
            hidden[s] = (gate / (1.0 + jnp.exp(-gate)) * lift).astype(jnp.bfloat16)

    def spread_hidden():
        slot_of = lax.broadcasted_iota(jnp.int32, (capacity, tables.shape[2]), 0).astype(jnp.float32)

        @pl.loop(0, sources)
        def _(b):
            code = tables[b, :8] - (e * 64).astype(jnp.float32)
            named = (code >= 0.0) & (code < 64.0)
            slot = jnp.sum(jnp.where(named, code + 1.0, 0.0), axis=0, keepdims=True) - 1.0
            weight = jnp.sum(jnp.where(named, tables[b, 8:], 0.0), axis=0, keepdims=True)
            onehot = (slot_of == slot).astype(jnp.bfloat16)
            inner = lax.rem(b, HALF)
            s = lax.div(inner, LINE) * (2 * LINE) + lax.rem(inner, LINE) * 2 + lax.div(b, HALF)
            picked = lax.dot_general(
                hidden[s], onehot, (((0,), (0,)), ((), ())), preferred_element_type=jnp.float32
            )
            lanes = pl.ds(pl.multiple_of(b * 128, 128), 128)
            spread[:, lanes] = (picked * weight).astype(jnp.bfloat16)

    def product(j):
        total = None
        step = 4
        for k in range(0, sources, step):
            part = rows[j, k : k + step].reshape(step * 128, COLS)
            term = jnp.dot(spread[:, k * 128 : (k + step) * 128], part, preferred_element_type=jnp.float32)
            total = term if total is None else total + term
        own[j] = total.astype(jnp.bfloat16)

    def finish(j):
        exchange(j).wait_recv()
        exchange(j).wait_send()
        both = own[j].astype(jnp.float32) + back[j].astype(jnp.float32)
        out_ref[:, pl.ds(pl.multiple_of(j * COLS, COLS), COLS)] = both.astype(jnp.bfloat16)

    def when_chunk(q, what):
        @pl.when((q >= 0) & (q < chunks))
        def _():
            what(rows.at[q], q)

    stages = (
        stage0,
        functools.partial(along_line, hop=1),
        functools.partial(along_line, hop=2),
        stage3,
        stage4,
        stage5,
        stage6,
    )
    quarter = sources // 4

    @pl.loop(0, chunks + 6 + RECV_LAG)
    def _(i):
        for k, stage in enumerate(stages):

            @pl.when(i == k)
            def _():
                if k == 0:
                    table_load.wait()
                stage(tables, TAB)

            if k == 0:

                @pl.when(i < chunks)
                def _():
                    load(i).wait()

            when_chunk(i - k, stage)

        @pl.when((i >= 1) & (i < 5))
        def _():
            @pl.when(i == 1)
            def _():
                pre_load.wait()

            make_hidden((i - 1) * quarter, quarter)

        @pl.when(i == 6)
        def _():
            spread_hidden()
            sent(tables, TAB)

        @pl.when((i >= 6) & (i - 6 < chunks))
        def _():
            product(i - 6)
            exchange(i - 6).start()
            sent(rows.at[i - 6], i - 6)

        @pl.when(i - 6 >= RECV_LAG)
        def _():
            finish(i - 6 - RECV_LAG)


def body(grad_out, expert_ids, slot_pos, gate_probs, saved_pre):
    grad_rows = grad_out[0]
    saved = saved_pre[0, :, 0]
    tokens, model = grad_rows.shape
    sources, capacity, both = saved.shape
    width = both // 2
    chunks = model // COLS
    code = jnp.where(slot_pos[0] >= 0, expert_ids[0] * 64 + slot_pos[0], -1).astype(jnp.float32)
    table = jnp.concatenate([code.T, gate_probs[0].T], axis=0)
    anywhere = pl.BlockSpec(memory_space=pl.ANY)
    result = pl.pallas_call(
        functools.partial(kernel, chunks, capacity),
        out_shape=jax.ShapeDtypeStruct((width, model), jnp.bfloat16),
        in_specs=[anywhere] * 3,
        out_specs=pl.BlockSpec(memory_space=pltpu.VMEM),
        scratch_shapes=[
            pltpu.VMEM((chunks, sources, tokens, COLS), jnp.bfloat16),
            pltpu.VMEM((sources, 16, tokens), jnp.float32),
            pltpu.VMEM((sources, capacity, both), jnp.bfloat16),
            pltpu.VMEM((sources, capacity, width), jnp.bfloat16),
            pltpu.VMEM((width, sources * tokens), jnp.bfloat16),
            pltpu.VMEM((chunks, width, COLS), jnp.bfloat16),
            pltpu.VMEM((chunks, width, COLS), jnp.bfloat16),
            pltpu.SemaphoreType.DMA((chunks + 1, 2, 3)),
            pltpu.SemaphoreType.DMA((chunks + 1, 2, 3)),
            pltpu.SemaphoreType.DMA((chunks + 1, 2, 2)),
            pltpu.SemaphoreType.DMA((chunks + 1, 2, 2)),
            pltpu.SemaphoreType.DMA((chunks + 1, 4)),
            pltpu.SemaphoreType.DMA((chunks + 1, 4)),
            pltpu.SemaphoreType.DMA((chunks,)),
            pltpu.SemaphoreType.DMA((chunks,)),
            pltpu.SemaphoreType.DMA((chunks,)),
            pltpu.SemaphoreType.DMA,
            pltpu.SemaphoreType.DMA,
        ],
        compiler_params=pltpu.CompilerParams(
            collective_id=0, has_side_effects=True, vmem_limit_bytes=52 * 1024 * 1024
        ),
        cost_estimate=pl.CostEstimate(
            flops=2 * sources * tokens * width * model,
            bytes_accessed=8 * 1024 * 1024,
            transcendentals=sources * capacity * width,
        ),
    )(table, grad_rows, saved)
    return result[None, None]


def solution(mesh):
    return jax.shard_map(
        body,
        mesh=mesh,
        in_specs=(
            P("pipe", "expert", None),
            P("pipe", "expert", None),
            P("pipe", "expert", None),
            P("pipe", "expert", None),
            P("pipe", None, "expert", None, None),
        ),
        out_specs=P("pipe", "expert", None, None),
        check_vma=False,
    )
```

```python
import functools

import jax
import jax.numpy as jnp
from jax import lax
from jax.experimental import pallas as pl
from jax.experimental.pallas import tpu as pltpu
from jax.sharding import PartitionSpec as P

MESH = pl.DeviceIdType.MESH
COLS = 128
RING = 4
SIDE = 4
LINE = 4
TOP = 8
DIRECT = 2
HALF = RING * LINE
RECV_LAG = 2
SECOND = 2
SINGLES = 4
ONE = {"start": (0, 0, 1, 2), "ring": 1, "pass": 2, "far": 3, "product": 4}
TWO = {"start": 2, "hop1": 3, "hop2": 4, "ring": 5, "pass": 6, "far": 7, "product": 8}


class Item:
    def __init__(self, buf, row, chunk=None, count=1):
        self.buf, self.row, self.chunk, self.count = buf, row, chunk, count

    def at(self, blocks):
        if self.chunk is None:
            return self.buf.at[blocks]
        if self.count == 1:
            return self.buf.at[self.chunk, blocks]
        return self.buf.at[pl.ds(self.chunk, self.count), blocks]


def kernel(
    chunks, capacity,
    ids_ref, slots_ref, gates_ref, grad_ref, saved_ref, out_ref,
    rows, tables, routing, weights, pre, hidden, hidden_out, hidden_in, turned, spread, spread_near,
    own, own_near, back, total_buf,
    z_send, z_recv, x_send, x_recv, s_send, s_recv, e_send, e_recv, n_send, n_recv, h_send, h_recv, load_sem, pre_sem, tab_sem, out_sem,
):
    e = lax.axis_index("expert")
    p = lax.axis_index("pipe")
    core = lax.rem(e, 2)
    zl = lax.rem(lax.div(e, 2), LINE)
    x = lax.div(e, 2 * LINE)
    x_left = lax.rem(x + RING - 1, RING)
    x_right = lax.rem(x + 1, RING)
    x_far = lax.rem(x + 2, RING)
    lane = zl * 2 + core
    flip = lax.rem(lax.div(p, SIDE), 2)
    away = 1 - 2 * flip
    d = zl + flip * (LINE - 1 - 2 * zl)
    near_e = e - 2 * away
    up = {"expert": e + 2 * away}
    down = {"expert": near_e}
    right = {"expert": x_right * 2 * LINE + lane}
    left = {"expert": x_left * 2 * LINE + lane}
    sibling = {"expert": e + 1 - 2 * core}
    mirror = {"pipe": lax.axis_size("pipe") - 1 - p}
    sources = tables.shape[0]
    width = spread.shape[0]
    pairs = (chunks - SINGLES) // 2
    table = Item(tables, SINGLES + pairs)

    def single(k):
        return Item(rows, k, k)

    def pair(j):
        return Item(rows, SINGLES + j, SINGLES + 2 * j, 2)

    def put(src, dst, ssem, rsem, where):
        return pltpu.make_async_remote_copy(
            src_ref=src, dst_ref=dst, send_sem=ssem, recv_sem=rsem, device_id=where, device_id_type=MESH
        )

    def block(it, place):
        return it.at(core * HALF + x * LINE + place + flip * (LINE - 1 - 2 * place))

    def column(it, xx, of, first=0, count=LINE):
        return it.at(pl.ds(of * HALF + xx * LINE + first, count))

    def load(j):
        return pltpu.make_async_copy(
            grad_ref.at[:, pl.ds(pl.multiple_of(j * COLS, COLS), COLS)],
            rows.at[j, core * HALF + x * LINE + zl],
            load_sem.at[j],
        )

    table_loads = [
        pltpu.make_async_copy(ids_ref, routing.at[0], tab_sem.at[0]),
        pltpu.make_async_copy(slots_ref, routing.at[1], tab_sem.at[1]),
        pltpu.make_async_copy(gates_ref, weights, tab_sem.at[2]),
    ]
    pre_load = pltpu.make_async_copy(saved_ref, pre, pre_sem.at[0])
    for one in table_loads:
        one.start()

    @pl.loop(0, chunks)
    def _(j):
        load(j).start()

    pre_load.start()

    barrier = pltpu.get_barrier_semaphore()
    for where in (right, left, sibling, mirror):
        pl.semaphore_signal(barrier, inc=1, device_id=where, device_id_type=MESH)

    for k in range(1, LINE):
        other = {"expert": x * 2 * LINE + lax.rem(zl + k, LINE) * 2 + core}
        pl.semaphore_signal(barrier, inc=1, device_id=other, device_id_type=MESH)

    for one in table_loads:
        one.wait()
    mine = core * HALF + x * LINE + zl
    tables[mine, :TOP] = jnp.where(routing[1] >= 0, routing[0] * 64 + routing[1], -1).astype(jnp.float32)
    tables[mine, TOP:] = weights[...]

    pl.semaphore_wait(barrier, 7)

    def go_up(it, hop):
        mine = block(it, d - hop)
        return put(mine, mine, z_send.at[it.row, 0, hop], z_recv.at[it.row, 0, hop], up)

    def go_down(it, hop):
        mine = block(it, d + hop)
        return put(mine, mine, z_send.at[it.row, 1, hop], z_recv.at[it.row, 1, hop], down)

    def go_right(it, hop):
        mine = column(it, x, core) if hop == 0 else column(it, x_left, core, 0, LINE // 2)
        return put(mine, mine, x_send.at[it.row, 0, hop], x_recv.at[it.row, 0, hop], right)

    def go_left(it, hop):
        mine = column(it, x, core) if hop == 0 else column(it, x_right, core, LINE // 2, LINE // 2)
        return put(mine, mine, x_send.at[it.row, 1, hop], x_recv.at[it.row, 1, hop], left)

    def go_across(it, k):
        mine = column(it, (x, x_left, x_right, x_far)[k], core)
        return put(mine, mine, s_send.at[it.row, k], s_recv.at[it.row, k], sibling)

    def await_up(it, hop):
        got = block(it, d - hop)
        put(got, got, z_send.at[it.row, 0, hop - 1], z_recv.at[it.row, 0, hop - 1], up).wait_recv()

    def await_down(it, hop):
        got = block(it, d + hop)
        put(got, got, z_send.at[it.row, 1, hop - 1], z_recv.at[it.row, 1, hop - 1], down).wait_recv()

    def await_right(it, hop):
        got = column(it, x_left, core) if hop == 0 else column(it, x_far, core, 0, LINE // 2)
        put(got, got, x_send.at[it.row, 0, hop], x_recv.at[it.row, 0, hop], right).wait_recv()

    def await_left(it, hop):
        got = column(it, x_right, core) if hop == 0 else column(it, x_far, core, LINE // 2, LINE // 2)
        put(got, got, x_send.at[it.row, 1, hop], x_recv.at[it.row, 1, hop], left).wait_recv()

    def await_across(it, k):
        got = column(it, (x, x_left, x_right, x_far)[k], 1 - core)
        put(got, got, s_send.at[it.row, k], s_recv.at[it.row, k], sibling).wait_recv()

    def direct_up(it, k):
        mine = block(it, d)
        return put(mine, mine, z_send.at[it.row, 0, k - 1], z_recv.at[it.row, 0, k - 1], {"expert": e + 2 * away * k})

    def direct_down(it, k):
        mine = block(it, d)
        return put(mine, mine, z_send.at[it.row, 1, k - 1], z_recv.at[it.row, 1, k - 1], {"expert": e - 2 * away * k})

    def direct(it, what):
        for k in range(1, LINE):

            @pl.when(d + k < LINE)
            def _():
                what(direct_up(it, k))

            @pl.when(d > k)
            def _():
                what(direct_down(it, k))

    def stage0_direct(it):
        direct(it, lambda copy: copy.start())

    def stage0(it):
        @pl.when(d < LINE - 1)
        def _():
            go_up(it, 0).start()

        @pl.when(d > 1)
        def _():
            go_down(it, 0).start()

    def along_line(it, hop):
        @pl.when(d >= hop)
        def _():
            await_up(it, hop)
            if hop < LINE - 1:

                @pl.when(d < LINE - 1)
                def _():
                    go_up(it, hop).start()

        @pl.when((d >= 1) & (d < LINE - hop))
        def _():
            await_down(it, hop)
            if hop < LINE - 1:

                @pl.when(d > 1)
                def _():
                    go_down(it, hop).start()

    def await_line(it):
        for hop in range(1, LINE):

            @pl.when(d >= hop)
            def _():
                await_up(it, hop)

            @pl.when((d >= 1) & (d < LINE - hop))
            def _():
                await_down(it, hop)

    def along_ring(it):
        go_right(it, 0).start()
        go_left(it, 0).start()
        go_across(it, 0).start()

    def stage4(it):
        await_right(it, 0)
        go_right(it, 1).start()
        go_across(it, 1).start()
        await_left(it, 0)
        go_left(it, 1).start()
        go_across(it, 2).start()

    def stage5(it):
        await_right(it, 1)
        await_left(it, 1)
        go_across(it, 3).start()

    def stage6(it):
        for k in range(4):
            await_across(it, k)

    def sent_line(it):
        for hop in range(LINE - 1):

            @pl.when((d >= hop) & (d < LINE - 1))
            def _():
                go_up(it, hop).wait_send()

            @pl.when((d < LINE - hop) & (d > 1))
            def _():
                go_down(it, hop).wait_send()

    def sent(it):
        for hop in range(2):
            go_right(it, hop).wait_send()
            go_left(it, hop).wait_send()
        for k in range(4):
            go_across(it, k).wait_send()

    def exchange(it):
        part = pl.ds(it.chunk, it.count)
        return put(own.at[part], back.at[part], e_send.at[it.row], e_recv.at[it.row], mirror)

    def hand_over(it):
        part = pl.ds(it.chunk, it.count)
        return put(own_near.at[part], own.at[part], n_send.at[it.row], n_recv.at[it.row], down)

    def lend():
        return put(hidden_out, hidden_in, h_send.at[0], h_recv.at[0], up)

    def make_hidden(part, parts):
        count = capacity // parts
        for k in range(count):
            c = part * count + k
            gate = pre[c, :, :width].astype(jnp.float32)
            lift = pre[c, :, width:].astype(jnp.float32)
            value = gate / (1.0 + jnp.exp(-gate)) * lift
            for half in range(width // 128):
                lanes = slice(half * 128, half * 128 + 128)
                at = pl.ds(pl.multiple_of(c * sources, sources), sources)
                hidden[half, at, :] = value[:, lanes]
                hidden_out[half, at, :] = value[:, lanes].astype(jnp.bfloat16)

    def turn_hidden(part, parts):
        count = sources // parts
        for k in range(count):
            s = part * count + k
            for half in range(width // 128):
                picked = hidden[half, pl.ds(s, capacity, stride=sources), :]
                turned[s, half * 128 : half * 128 + 128] = picked.T.astype(jnp.bfloat16)

    def spread_column(xx, of, spread=spread, expert=e):
        slot_of = lax.broadcasted_iota(jnp.int32, (capacity, tables.shape[2]), 0).astype(jnp.float32)
        first = (expert * 64).astype(jnp.float32)
        for zz in range(LINE):
            b = of * HALF + xx * LINE + zz
            code = tables[b, :TOP] - first
            named = (code >= 0.0) & (code < 64.0)
            slot = jnp.sum(jnp.where(named, code + 1.0, 0.0), axis=0, keepdims=True) - 1.0
            weight = jnp.sum(jnp.where(named, tables[b, TOP:], 0.0), axis=0, keepdims=True)
            onehot = (slot_of == slot).astype(jnp.bfloat16)
            picked = jnp.dot(
                turned[xx * (2 * LINE) + zz * 2 + of], onehot, preferred_element_type=jnp.float32
            )
            lanes = pl.ds(pl.multiple_of(b * 128, 128), 128)
            spread[:, lanes] = (picked * weight).astype(jnp.bfloat16)

    def product(it, spread, own):
        total = None
        step = 4
        for k in range(0, sources, step):
            parts = [rows[it.chunk + c, k : k + step].reshape(step * 128, COLS) for c in range(it.count)]
            part = parts[0] if it.count == 1 else jnp.concatenate(parts, axis=1)
            term = jnp.dot(spread[:, k * 128 : (k + step) * 128], part, preferred_element_type=jnp.float32)
            total = term if total is None else total + term
        for c in range(it.count):
            own[it.chunk + c] = total[:, c * COLS : (c + 1) * COLS].astype(jnp.bfloat16)

    def store(it):
        lanes = pl.ds(pl.multiple_of(it.chunk * COLS, COLS), it.count * COLS)
        return pltpu.make_async_copy(total_buf.at[:, lanes], out_ref.at[:, lanes], out_sem.at[it.row])

    def finish(it):
        exchange(it).wait_recv()
        exchange(it).wait_send()

        @pl.when(d == 1)
        def _():
            hand_over(it).wait_send()

        for c in range(it.count):
            j = it.chunk + c
            both = own[j].astype(jnp.float32) + back[j].astype(jnp.float32)
            total_buf[:, pl.ds(pl.multiple_of(j * COLS, COLS), COLS)] = both.astype(jnp.bfloat16)
        store(it).start()

    def relay(it):
        hand_over(it).wait_recv()
        exchange(it).start()

    def multiply_near(it):
        product(it, spread_near, own_near)
        hand_over(it).start()

    def multiply(it):
        stage6(it)
        product(it, spread, own)
        exchange(it).start()

    def multiply_two(it):
        stage6(it)

        @pl.when(d == 1)
        def _():
            multiply_near(it)

        product(it, spread, own)
        exchange(it).start()

    def loaded(it):
        for c in range(it.count):
            load(it.chunk + c).wait()

    @pl.loop(0, pairs + TWO["product"] + RECV_LAG)
    def _(i):
        gathers = d >= 1
        always = d >= 0

        def at_step(who, step, what, *args):
            @pl.when((i == step) & who)
            def _():
                what(*args)

        def of_pair(who, step, what, *args):
            @pl.when((i >= step) & (i < step + pairs) & who)
            def _():
                what(pair(i - step), *args)

        def ring_of(it):
            await_line(it)
            along_ring(it)

        def start_single(it):
            loaded(it)
            stage0_direct(it)

        def start_pair(it):
            loaded(it)
            stage0(it)

        def last_hop(it):
            along_line(it, 3)
            along_ring(it)

        def hide():
            pre_load.wait()
            pl.loop(0, 9)(lambda part: make_hidden(part, 9))

        def turn():
            pl.loop(0, 8)(lambda part: turn_hidden(part, 8))

        def spread_some(waits, columns):
            for k in waits:
                await_across(table, k)
            for column_of in columns:
                spread_column(*column_of)

        def borrow():
            lend().wait_recv()
            for half in range(width // 128):
                hidden[half] = hidden_in[half].astype(jnp.float32)
            turn()

            @pl.loop(0, RING)
            def _(k):
                spread_column(k, core, spread_near, near_e)
                spread_column(k, 1 - core, spread_near, near_e)

        def done_line(it):
            direct(it, lambda copy: copy.wait_send())

        at_step(always, 0, stage0_direct, table)
        at_step(gathers, 1, ring_of, table)
        at_step(gathers, 2, stage4, table)
        at_step(gathers, 3, stage5, table)
        for k in range(SINGLES):
            at_step(always, ONE["start"][k], start_single, single(k))
        for k in range(SINGLES):
            at_step(gathers, k + ONE["pass"], stage4, single(k))
        for k in range(SINGLES):
            at_step(gathers, k + ONE["ring"], ring_of, single(k))
        for k in range(SINGLES):
            at_step(gathers, k + ONE["far"], stage5, single(k))

        of_pair(always, TWO["start"], start_pair)
        of_pair(gathers, TWO["hop1"], along_line, 1)
        of_pair(gathers, TWO["hop2"], along_line, 2)
        of_pair(gathers, TWO["ring"], last_hop)
        of_pair(gathers, TWO["pass"], stage4)
        of_pair(gathers, TWO["far"], stage5)

        at_step(always, 0, hide)
        at_step(d == 0, 0, lambda: lend().start())
        at_step(gathers, 1, turn)
        at_step(gathers, 2, spread_some, (), ((x, core),))
        at_step(gathers, 3, spread_some, (0,), ((x, 1 - core), (x_left, core), (x_right, core)))
        rest = ((x_left, 1 - core), (x_right, 1 - core), (x_far, core), (x_far, 1 - core))
        at_step(gathers, 4, spread_some, (1, 2, 3), rest)

        for k in range(SINGLES):
            at_step(gathers, k + ONE["product"], multiply, single(k))
        at_step(d == 1, ONE["product"] + SECOND, borrow)
        for k in range(SINGLES):
            at_step(d == 1, k + ONE["product"] + SECOND, multiply_near, single(k))
        of_pair(gathers, TWO["product"], multiply_two)

        at_step(always, 6, done_line, table)
        at_step(gathers, 6, sent, table)
        at_step(d == 0, 6, lambda: lend().wait_send())
        for k in range(SINGLES):
            at_step(always, k + ONE["product"] + 1, done_line, single(k))
            at_step(gathers, k + ONE["product"] + 1, sent, single(k))
        of_pair(always, TWO["product"], sent_line)
        of_pair(gathers, TWO["product"], sent)
        for k in range(SINGLES):
            at_step(d == 0, k + ONE["product"] + SECOND + 1, relay, single(k))
        of_pair(d == 0, TWO["product"] + 1, relay)
        for k in range(SINGLES):
            at_step(always, k + TWO["product"] + 1, finish, single(k))
        of_pair(always, TWO["product"] + RECV_LAG, finish)

    for k in range(SINGLES):
        store(single(k)).wait()

    @pl.loop(0, pairs)
    def _(j):
        store(pair(j)).wait()


def body(grad_out, expert_ids, slot_pos, gate_probs, saved_pre):
    grad_rows = grad_out[0]
    saved = saved_pre[0, :, 0].transpose(1, 0, 2)
    tokens, model = grad_rows.shape
    capacity, sources, both = saved.shape
    width = both // 2
    chunks = model // COLS
    items = SINGLES + (chunks - SINGLES) // 2
    semaphores = (
        [(items + 1, 2, 3)] * 2 + [(items + 1, 2, 2)] * 2 + [(items + 1, 4)] * 2 + [(items,)] * 2
        + [(items,), (items,), (1,), (1,), (chunks,), (1,), (3,), (items,)]
    )
    anywhere = pl.BlockSpec(memory_space=pl.ANY)
    result = pl.pallas_call(
        functools.partial(kernel, chunks, capacity),
        out_shape=jax.ShapeDtypeStruct((width, model), jnp.bfloat16),
        in_specs=[anywhere] * 5,
        out_specs=anywhere,
        scratch_shapes=[
            pltpu.VMEM((chunks, sources, tokens, COLS), jnp.bfloat16),
            pltpu.VMEM((sources, 16, tokens), jnp.float32),
            pltpu.VMEM((2, TOP, tokens), jnp.int32),
            pltpu.VMEM((TOP, tokens), jnp.float32),
            pltpu.VMEM((capacity, sources, both), jnp.bfloat16),
            pltpu.VMEM((width // 128, capacity * sources, 128), jnp.float32),
            pltpu.VMEM((width // 128, capacity * sources, 128), jnp.bfloat16),
            pltpu.VMEM((width // 128, capacity * sources, 128), jnp.bfloat16),
            pltpu.VMEM((sources, width, capacity), jnp.bfloat16),
            pltpu.VMEM((width, sources * tokens), jnp.bfloat16),
            pltpu.VMEM((width, sources * tokens), jnp.bfloat16),
            pltpu.VMEM((chunks, width, COLS), jnp.bfloat16),
            pltpu.VMEM((chunks, width, COLS), jnp.bfloat16),
            pltpu.VMEM((chunks, width, COLS), jnp.bfloat16),
            pltpu.VMEM((width, model), jnp.bfloat16),
            *[pltpu.SemaphoreType.DMA(shape) for shape in semaphores],
        ],
        compiler_params=pltpu.CompilerParams(
            collective_id=0, has_side_effects=True, vmem_limit_bytes=62 * 1024 * 1024
        ),
        cost_estimate=pl.CostEstimate(
            flops=2 * sources * tokens * width * model,
            bytes_accessed=8 * 1024 * 1024,
            transcendentals=sources * capacity * width,
        ),
    )(expert_ids[0].T, slot_pos[0].T, gate_probs[0].T, grad_rows, saved)
    return result[None, None]


def solution(mesh):
    return jax.shard_map(
        body,
        mesh=mesh,
        in_specs=(
            P("pipe", "expert", None),
            P("pipe", "expert", None),
            P("pipe", "expert", None),
            P("pipe", "expert", None),
            P("pipe", None, "expert", None, None),
        ),
        out_specs=P("pipe", "expert", None, None),
        check_vma=False,
    )
```

```python
import functools

import jax
import jax.numpy as jnp
from jax import lax
from jax.experimental import pallas as pl
from jax.experimental.pallas import tpu as pltpu
from jax.sharding import PartitionSpec as P

MESH = pl.DeviceIdType.MESH
COLS = 128
RING = 4
SIDE = 4
LINE = 4
TOP = 8
DIRECT = 2
HALF = RING * LINE
RECV_LAG = 2
BORROW = 6
SINGLES = 4
ONE = {"start": (0, 0, 1, 2), "ring": 1, "pass": 2, "far": 3, "product": 4}
TWO = {"start": 2, "hop1": 3, "hop2": 4, "ring": 5, "pass": 6, "far": 7, "product": 8}


class Item:
    def __init__(self, buf, row, chunk=None, count=1):
        self.buf, self.row, self.chunk, self.count = buf, row, chunk, count

    def at(self, blocks):
        if self.chunk is None:
            return self.buf.at[blocks]
        if self.count == 1:
            return self.buf.at[self.chunk, blocks]
        return self.buf.at[pl.ds(self.chunk, self.count), blocks]


def kernel(
    chunks, capacity,
    ids_ref, slots_ref, gates_ref, grad_ref, saved_ref, out_ref,
    rows, tables, routing, weights, pre, hidden, hidden_out, hidden_in, turned, spread, spread_near,
    own, own_near, back, total_buf,
    z_send, z_recv, x_send, x_recv, s_send, s_recv, e_send, e_recv, n_send, n_recv, h_send, h_recv, load_sem, pre_sem, tab_sem, out_sem,
):
    e = lax.axis_index("expert")
    p = lax.axis_index("pipe")
    core = lax.rem(e, 2)
    zl = lax.rem(lax.div(e, 2), LINE)
    x = lax.div(e, 2 * LINE)
    x_left = lax.rem(x + RING - 1, RING)
    x_right = lax.rem(x + 1, RING)
    x_far = lax.rem(x + 2, RING)
    lane = zl * 2 + core
    flip = lax.rem(lax.div(p, SIDE), 2)
    away = 1 - 2 * flip
    d = zl + flip * (LINE - 1 - 2 * zl)
    near_e = e - 2 * away
    up = {"expert": e + 2 * away}
    down = {"expert": near_e}
    right = {"expert": x_right * 2 * LINE + lane}
    left = {"expert": x_left * 2 * LINE + lane}
    sibling = {"expert": e + 1 - 2 * core}
    mirror = {"pipe": lax.axis_size("pipe") - 1 - p}
    sources = tables.shape[0]
    width = spread.shape[0]
    pairs = (chunks - SINGLES) // 2
    table = Item(tables, SINGLES + pairs)

    def single(k):
        return Item(rows, k, k)

    def pair(j):
        return Item(rows, SINGLES + j, SINGLES + 2 * j, 2)

    def put(src, dst, ssem, rsem, where):
        return pltpu.make_async_remote_copy(
            src_ref=src, dst_ref=dst, send_sem=ssem, recv_sem=rsem, device_id=where, device_id_type=MESH
        )

    def block(it, place):
        return it.at(core * HALF + x * LINE + place + flip * (LINE - 1 - 2 * place))

    def column(it, xx, of, first=0, count=LINE):
        return it.at(pl.ds(of * HALF + xx * LINE + first, count))

    def load(j):
        return pltpu.make_async_copy(
            grad_ref.at[:, pl.ds(pl.multiple_of(j * COLS, COLS), COLS)],
            rows.at[j, core * HALF + x * LINE + zl],
            load_sem.at[j],
        )

    table_loads = [
        pltpu.make_async_copy(ids_ref, routing.at[0], tab_sem.at[0]),
        pltpu.make_async_copy(slots_ref, routing.at[1], tab_sem.at[1]),
        pltpu.make_async_copy(gates_ref, weights, tab_sem.at[2]),
    ]
    pre_load = pltpu.make_async_copy(saved_ref, pre, pre_sem.at[0])
    for one in table_loads:
        one.start()

    @pl.loop(0, chunks)
    def _(j):
        load(j).start()

    pre_load.start()

    barrier = pltpu.get_barrier_semaphore()
    for where in (right, left, sibling, mirror):
        pl.semaphore_signal(barrier, inc=1, device_id=where, device_id_type=MESH)

    for k in range(1, LINE):
        other = {"expert": x * 2 * LINE + lax.rem(zl + k, LINE) * 2 + core}
        pl.semaphore_signal(barrier, inc=1, device_id=other, device_id_type=MESH)

    for one in table_loads:
        one.wait()
    mine = core * HALF + x * LINE + zl
    tables[mine, :TOP] = jnp.where(routing[1] >= 0, routing[0] * 64 + routing[1], -1).astype(jnp.float32)
    tables[mine, TOP:] = weights[...]

    pl.semaphore_wait(barrier, 7)

    def go_up(it, hop):
        mine = block(it, d - hop)
        return put(mine, mine, z_send.at[it.row, 0, hop], z_recv.at[it.row, 0, hop], up)

    def go_down(it, hop):
        mine = block(it, d + hop)
        return put(mine, mine, z_send.at[it.row, 1, hop], z_recv.at[it.row, 1, hop], down)

    def go_right(it, hop):
        mine = column(it, x, core) if hop == 0 else column(it, x_left, core, 0, LINE // 2)
        return put(mine, mine, x_send.at[it.row, 0, hop], x_recv.at[it.row, 0, hop], right)

    def go_left(it, hop):
        mine = column(it, x, core) if hop == 0 else column(it, x_right, core, LINE // 2, LINE // 2)
        return put(mine, mine, x_send.at[it.row, 1, hop], x_recv.at[it.row, 1, hop], left)

    def go_across(it, k):
        mine = column(it, (x, x_left, x_right, x_far)[k], core)
        return put(mine, mine, s_send.at[it.row, k], s_recv.at[it.row, k], sibling)

    def await_up(it, hop):
        got = block(it, d - hop)
        put(got, got, z_send.at[it.row, 0, hop - 1], z_recv.at[it.row, 0, hop - 1], up).wait_recv()

    def await_down(it, hop):
        got = block(it, d + hop)
        put(got, got, z_send.at[it.row, 1, hop - 1], z_recv.at[it.row, 1, hop - 1], down).wait_recv()

    def await_right(it, hop):
        got = column(it, x_left, core) if hop == 0 else column(it, x_far, core, 0, LINE // 2)
        put(got, got, x_send.at[it.row, 0, hop], x_recv.at[it.row, 0, hop], right).wait_recv()

    def await_left(it, hop):
        got = column(it, x_right, core) if hop == 0 else column(it, x_far, core, LINE // 2, LINE // 2)
        put(got, got, x_send.at[it.row, 1, hop], x_recv.at[it.row, 1, hop], left).wait_recv()

    def await_across(it, k):
        got = column(it, (x, x_left, x_right, x_far)[k], 1 - core)
        put(got, got, s_send.at[it.row, k], s_recv.at[it.row, k], sibling).wait_recv()

    def direct_up(it, k):
        mine = block(it, d)
        return put(mine, mine, z_send.at[it.row, 0, k - 1], z_recv.at[it.row, 0, k - 1], {"expert": e + 2 * away * k})

    def direct_down(it, k):
        mine = block(it, d)
        return put(mine, mine, z_send.at[it.row, 1, k - 1], z_recv.at[it.row, 1, k - 1], {"expert": e - 2 * away * k})

    def direct(it, what):
        for k in range(1, LINE):

            @pl.when(d + k < LINE)
            def _():
                what(direct_up(it, k))

            @pl.when(d >= k)
            def _():
                what(direct_down(it, k))

    def stage0_direct(it):
        direct(it, lambda copy: copy.start())

    def stage0(it):
        @pl.when(d < LINE - 1)
        def _():
            go_up(it, 0).start()

        @pl.when(d > 1)
        def _():
            go_down(it, 0).start()

    def along_line(it, hop):
        @pl.when(d >= hop)
        def _():
            await_up(it, hop)
            if hop < LINE - 1:

                @pl.when(d < LINE - 1)
                def _():
                    go_up(it, hop).start()

        @pl.when((d >= 1) & (d < LINE - hop))
        def _():
            await_down(it, hop)
            if hop < LINE - 1:

                @pl.when(d > 1)
                def _():
                    go_down(it, hop).start()

    def await_line(it):
        for hop in range(1, LINE):

            @pl.when(d >= hop)
            def _():
                await_up(it, hop)

            @pl.when(d < LINE - hop)
            def _():
                await_down(it, hop)

    def along_ring(it):
        go_right(it, 0).start()
        go_left(it, 0).start()
        go_across(it, 0).start()

    def stage4(it):
        await_right(it, 0)
        go_right(it, 1).start()
        go_across(it, 1).start()
        await_left(it, 0)
        go_left(it, 1).start()
        go_across(it, 2).start()

    def stage5(it):
        await_right(it, 1)
        await_left(it, 1)
        go_across(it, 3).start()

    def stage6(it):
        for k in range(4):
            await_across(it, k)

    def sent_line(it):
        for hop in range(LINE - 1):

            @pl.when((d >= hop) & (d < LINE - 1))
            def _():
                go_up(it, hop).wait_send()

            @pl.when((d < LINE - hop) & (d > 1))
            def _():
                go_down(it, hop).wait_send()

    def sent(it):
        for hop in range(2):
            go_right(it, hop).wait_send()
            go_left(it, hop).wait_send()
        for k in range(4):
            go_across(it, k).wait_send()

    def exchange(it):
        part = pl.ds(it.chunk, it.count)
        return put(own.at[part], back.at[part], e_send.at[it.row], e_recv.at[it.row], mirror)

    def hand_over(it):
        part = pl.ds(it.chunk, it.count)
        return put(own_near.at[part], own.at[part], n_send.at[it.row], n_recv.at[it.row], down)

    def lend():
        return put(hidden_out, hidden_in, h_send.at[0], h_recv.at[0], up)

    def make_hidden(part, parts):
        count = capacity // parts
        for k in range(count):
            c = part * count + k
            gate = pre[c, :, :width].astype(jnp.float32)
            lift = pre[c, :, width:].astype(jnp.float32)
            value = gate / (1.0 + jnp.exp(-gate)) * lift
            for half in range(width // 128):
                lanes = slice(half * 128, half * 128 + 128)
                at = pl.ds(pl.multiple_of(c * sources, sources), sources)
                hidden[half, at, :] = value[:, lanes]
                hidden_out[half, at, :] = value[:, lanes].astype(jnp.bfloat16)

    def turn_hidden(part, parts):
        count = sources // parts
        for k in range(count):
            s = part * count + k
            for half in range(width // 128):
                picked = hidden[half, pl.ds(s, capacity, stride=sources), :]
                turned[s, half * 128 : half * 128 + 128] = picked.T.astype(jnp.bfloat16)

    def spread_column(xx, of, spread=spread, expert=e):
        slot_of = lax.broadcasted_iota(jnp.int32, (capacity, tables.shape[2]), 0).astype(jnp.float32)
        first = (expert * 64).astype(jnp.float32)
        for zz in range(LINE):
            b = of * HALF + xx * LINE + zz
            code = tables[b, :TOP] - first
            named = (code >= 0.0) & (code < 64.0)
            slot = jnp.sum(jnp.where(named, code + 1.0, 0.0), axis=0, keepdims=True) - 1.0
            weight = jnp.sum(jnp.where(named, tables[b, TOP:], 0.0), axis=0, keepdims=True)
            onehot = (slot_of == slot).astype(jnp.bfloat16)
            picked = jnp.dot(
                turned[xx * (2 * LINE) + zz * 2 + of], onehot, preferred_element_type=jnp.float32
            )
            lanes = pl.ds(pl.multiple_of(b * 128, 128), 128)
            spread[:, lanes] = (picked * weight).astype(jnp.bfloat16)

    def product(it, spread, own):
        total = None
        step = 4
        for k in range(0, sources, step):
            parts = [rows[it.chunk + c, k : k + step].reshape(step * 128, COLS) for c in range(it.count)]
            part = parts[0] if it.count == 1 else jnp.concatenate(parts, axis=1)
            term = jnp.dot(spread[:, k * 128 : (k + step) * 128], part, preferred_element_type=jnp.float32)
            total = term if total is None else total + term
        for c in range(it.count):
            own[it.chunk + c] = total[:, c * COLS : (c + 1) * COLS].astype(jnp.bfloat16)

    def store(it):
        lanes = pl.ds(pl.multiple_of(it.chunk * COLS, COLS), it.count * COLS)
        return pltpu.make_async_copy(total_buf.at[:, lanes], out_ref.at[:, lanes], out_sem.at[it.row])

    def finish(it):
        exchange(it).wait_recv()
        exchange(it).wait_send()
        if it.count == 2:

            @pl.when(d == 1)
            def _():
                hand_over(it).wait_send()

        for c in range(it.count):
            j = it.chunk + c
            both = own[j].astype(jnp.float32) + back[j].astype(jnp.float32)
            total_buf[:, pl.ds(pl.multiple_of(j * COLS, COLS), COLS)] = both.astype(jnp.bfloat16)
        store(it).start()

    def relay(it):
        hand_over(it).wait_recv()
        exchange(it).start()

    def multiply_near(it):
        product(it, spread_near, own_near)
        hand_over(it).start()

    def multiply(it):
        stage6(it)
        product(it, spread, own)
        exchange(it).start()

    def multiply_two(it):
        stage6(it)

        @pl.when(d == 1)
        def _():
            multiply_near(it)

        product(it, spread, own)
        exchange(it).start()

    def loaded(it):
        for c in range(it.count):
            load(it.chunk + c).wait()

    @pl.loop(0, pairs + TWO["product"] + RECV_LAG)
    def _(i):
        gathers = d >= 1
        always = d >= 0

        def at_step(who, step, what, *args):
            @pl.when((i == step) & who)
            def _():
                what(*args)

        def of_pair(who, step, what, *args):
            @pl.when((i >= step) & (i < step + pairs) & who)
            def _():
                what(pair(i - step), *args)

        def ring_of(it):
            await_line(it)
            along_ring(it)

        def start_single(it):
            loaded(it)
            stage0_direct(it)

        def start_pair(it):
            loaded(it)
            stage0(it)

        def last_hop(it):
            along_line(it, 3)
            along_ring(it)

        def hide():
            pre_load.wait()
            pl.loop(0, 9)(lambda part: make_hidden(part, 9))

        def turn():
            pl.loop(0, 8)(lambda part: turn_hidden(part, 8))

        def spread_some(waits, columns):
            for k in waits:
                await_across(table, k)
            for column_of in columns:
                spread_column(*column_of)

        def borrow():
            lend().wait_recv()
            for half in range(width // 128):
                hidden[half] = hidden_in[half].astype(jnp.float32)
            turn()

            @pl.loop(0, RING)
            def _(k):
                spread_column(k, core, spread_near, near_e)
                spread_column(k, 1 - core, spread_near, near_e)

        def done_line(it):
            direct(it, lambda copy: copy.wait_send())

        of_pair(gathers, TWO["product"], multiply_two)

        at_step(always, 0, stage0_direct, table)
        at_step(always, 1, ring_of, table)
        at_step(always, 2, stage4, table)
        at_step(always, 3, stage5, table)
        for k in range(SINGLES):
            at_step(always, ONE["start"][k], start_single, single(k))
        for k in range(SINGLES):
            at_step(always, k + ONE["pass"], stage4, single(k))
        for k in range(SINGLES):
            at_step(always, k + ONE["ring"], ring_of, single(k))
        for k in range(SINGLES):
            at_step(always, k + ONE["far"], stage5, single(k))

        of_pair(gathers, TWO["far"], stage5)
        of_pair(gathers, TWO["pass"], stage4)
        of_pair(gathers, TWO["ring"], last_hop)
        of_pair(gathers, TWO["hop2"], along_line, 2)
        of_pair(gathers, TWO["hop1"], along_line, 1)
        of_pair(always, TWO["start"], start_pair)

        at_step(always, 0, hide)
        at_step(d == 0, 0, lambda: lend().start())
        at_step(always, 1, turn)
        at_step(always, 2, spread_some, (), ((x, core),))
        at_step(always, 3, spread_some, (0,), ((x, 1 - core), (x_left, core), (x_right, core)))
        rest = ((x_left, 1 - core), (x_right, 1 - core), (x_far, core), (x_far, 1 - core))
        at_step(always, 4, spread_some, (1, 2, 3), rest)

        for k in range(SINGLES):
            at_step(always, k + ONE["product"], multiply, single(k))
        at_step(d == 1, BORROW, borrow)

        at_step(always, 6, done_line, table)
        at_step(always, 6, sent, table)
        at_step(d == 0, 6, lambda: lend().wait_send())
        for k in range(SINGLES):
            at_step(always, k + ONE["product"] + 1, done_line, single(k))
            at_step(always, k + ONE["product"] + 1, sent, single(k))
        of_pair(always, TWO["product"], sent_line)
        of_pair(gathers, TWO["product"], sent)
        of_pair(d == 0, TWO["product"] + 1, relay)
        for k in range(SINGLES):
            at_step(always, k + TWO["product"] + 1, finish, single(k))
        of_pair(always, TWO["product"] + RECV_LAG, finish)

    for k in range(SINGLES):
        store(single(k)).wait()

    @pl.loop(0, pairs)
    def _(j):
        store(pair(j)).wait()


def body(grad_out, expert_ids, slot_pos, gate_probs, saved_pre):
    grad_rows = grad_out[0]
    saved = saved_pre[0, :, 0].transpose(1, 0, 2)
    tokens, model = grad_rows.shape
    capacity, sources, both = saved.shape
    width = both // 2
    chunks = model // COLS
    items = SINGLES + (chunks - SINGLES) // 2
    semaphores = (
        [(items + 1, 2, 3)] * 2 + [(items + 1, 2, 2)] * 2 + [(items + 1, 4)] * 2 + [(items,)] * 2
        + [(items,), (items,), (1,), (1,), (chunks,), (1,), (3,), (items,)]
    )
    anywhere = pl.BlockSpec(memory_space=pl.ANY)
    result = pl.pallas_call(
        functools.partial(kernel, chunks, capacity),
        out_shape=jax.ShapeDtypeStruct((width, model), jnp.bfloat16),
        in_specs=[anywhere] * 5,
        out_specs=anywhere,
        scratch_shapes=[
            pltpu.VMEM((chunks, sources, tokens, COLS), jnp.bfloat16),
            pltpu.VMEM((sources, 16, tokens), jnp.float32),
            pltpu.VMEM((2, TOP, tokens), jnp.int32),
            pltpu.VMEM((TOP, tokens), jnp.float32),
            pltpu.VMEM((capacity, sources, both), jnp.bfloat16),
            pltpu.VMEM((width // 128, capacity * sources, 128), jnp.float32),
            pltpu.VMEM((width // 128, capacity * sources, 128), jnp.bfloat16),
            pltpu.VMEM((width // 128, capacity * sources, 128), jnp.bfloat16),
            pltpu.VMEM((sources, width, capacity), jnp.bfloat16),
            pltpu.VMEM((width, sources * tokens), jnp.bfloat16),
            pltpu.VMEM((width, sources * tokens), jnp.bfloat16),
            pltpu.VMEM((chunks, width, COLS), jnp.bfloat16),
            pltpu.VMEM((chunks, width, COLS), jnp.bfloat16),
            pltpu.VMEM((chunks, width, COLS), jnp.bfloat16),
            pltpu.VMEM((width, model), jnp.bfloat16),
            *[pltpu.SemaphoreType.DMA(shape) for shape in semaphores],
        ],
        compiler_params=pltpu.CompilerParams(
            collective_id=0, has_side_effects=True, vmem_limit_bytes=62 * 1024 * 1024
        ),
        cost_estimate=pl.CostEstimate(
            flops=2 * sources * tokens * width * model,
            bytes_accessed=8 * 1024 * 1024,
            transcendentals=sources * capacity * width,
        ),
    )(expert_ids[0].T, slot_pos[0].T, gate_probs[0].T, grad_rows, saved)
    return result[None, None]


def solution(mesh):
    return jax.shard_map(
        body,
        mesh=mesh,
        in_specs=(
            P("pipe", "expert", None),
            P("pipe", "expert", None),
            P("pipe", "expert", None),
            P("pipe", "expert", None),
            P("pipe", None, "expert", None, None),
        ),
        out_specs=P("pipe", "expert", None, None),
        check_vma=False,
    )
```

```python
import functools

import jax
import jax.numpy as jnp
from jax import lax
from jax.experimental import pallas as pl
from jax.experimental.pallas import tpu as pltpu
from jax.sharding import PartitionSpec as P

MESH = pl.DeviceIdType.MESH
COLS = 128
RING = 4
SIDE = 4
LINE = 4
TOP = 8
DIRECT = 2
HALF = RING * LINE
RECV_LAG = 2
BORROW = 6
SINGLES = 4
ONE = {"start": (0, 0, 1, 2), "ring": 1, "pass": 2, "far": 3, "product": 4}
TWO = {"start": 2, "hop1": 3, "hop2": 4, "ring": 5, "pass": 6, "far": 7, "product": 8}


class Item:
    def __init__(self, buf, row, chunk=None, count=1):
        self.buf, self.row, self.chunk, self.count = buf, row, chunk, count

    def at(self, blocks):
        if self.chunk is None:
            return self.buf.at[blocks]
        if self.count == 1:
            return self.buf.at[self.chunk, blocks]
        return self.buf.at[pl.ds(self.chunk, self.count), blocks]


def kernel(
    chunks, capacity,
    ids_ref, slots_ref, gates_ref, grad_ref, saved_ref, out_ref,
    rows, tables, routing, weights, pre, hidden, hidden_out, hidden_in, turned, spread, spread_near,
    own, own_near, back, total_buf,
    z_send, z_recv, x_send, x_recv, s_send, s_recv, e_send, e_recv, n_send, n_recv, h_send, h_recv, load_sem, pre_sem, tab_sem, out_sem,
):
    e = lax.axis_index("expert")
    p = lax.axis_index("pipe")
    core = lax.rem(e, 2)
    zl = lax.rem(lax.div(e, 2), LINE)
    x = lax.div(e, 2 * LINE)
    x_left = lax.rem(x + RING - 1, RING)
    x_right = lax.rem(x + 1, RING)
    x_far = lax.rem(x + 2, RING)
    lane = zl * 2 + core
    flip = lax.rem(lax.div(p, SIDE), 2)
    away = 1 - 2 * flip
    d = zl + flip * (LINE - 1 - 2 * zl)
    near_e = e - 2 * away
    up = {"expert": e + 2 * away}
    down = {"expert": near_e}
    right = {"expert": x_right * 2 * LINE + lane}
    left = {"expert": x_left * 2 * LINE + lane}
    sibling = {"expert": e + 1 - 2 * core}
    mirror = {"pipe": lax.axis_size("pipe") - 1 - p}
    sources = tables.shape[0]
    width = spread.shape[0]
    pairs = (chunks - SINGLES) // 2
    table = Item(tables, SINGLES + pairs)

    def single(k):
        return Item(rows, k, k)

    def pair(j):
        return Item(rows, SINGLES + j, SINGLES + 2 * j, 2)

    def put(src, dst, ssem, rsem, where):
        return pltpu.make_async_remote_copy(
            src_ref=src, dst_ref=dst, send_sem=ssem, recv_sem=rsem, device_id=where, device_id_type=MESH
        )

    def block(it, place):
        return it.at(core * HALF + x * LINE + place + flip * (LINE - 1 - 2 * place))

    def column(it, xx, of, first=0, count=LINE):
        return it.at(pl.ds(of * HALF + xx * LINE + first, count))

    def load(j):
        return pltpu.make_async_copy(
            grad_ref.at[:, pl.ds(pl.multiple_of(j * COLS, COLS), COLS)],
            rows.at[j, core * HALF + x * LINE + zl],
            load_sem.at[j],
        )

    table_loads = [
        pltpu.make_async_copy(ids_ref, routing.at[0], tab_sem.at[0]),
        pltpu.make_async_copy(slots_ref, routing.at[1], tab_sem.at[1]),
        pltpu.make_async_copy(gates_ref, weights, tab_sem.at[2]),
    ]
    pre_load = pltpu.make_async_copy(saved_ref, pre, pre_sem.at[0])
    for one in table_loads:
        one.start()

    @pl.loop(0, chunks)
    def _(j):
        load(j).start()

    pre_load.start()

    barrier = pltpu.get_barrier_semaphore()
    for where in (right, left, sibling, mirror):
        pl.semaphore_signal(barrier, inc=1, device_id=where, device_id_type=MESH)

    for k in range(1, LINE):
        other = {"expert": x * 2 * LINE + lax.rem(zl + k, LINE) * 2 + core}
        pl.semaphore_signal(barrier, inc=1, device_id=other, device_id_type=MESH)

    for one in table_loads:
        one.wait()
    mine = core * HALF + x * LINE + zl
    tables[mine, :TOP] = jnp.where(routing[1] >= 0, routing[0] * 64 + routing[1], -1).astype(jnp.float32)
    tables[mine, TOP:] = weights[...]

    pl.semaphore_wait(barrier, 7)

    def go_up(it, hop):
        mine = block(it, d - hop)
        return put(mine, mine, z_send.at[it.row, 0, hop], z_recv.at[it.row, 0, hop], up)

    def go_down(it, hop):
        mine = block(it, d + hop)
        return put(mine, mine, z_send.at[it.row, 1, hop], z_recv.at[it.row, 1, hop], down)

    def go_right(it, hop):
        mine = column(it, x, core) if hop == 0 else column(it, x_left, core, 0, LINE // 2)
        return put(mine, mine, x_send.at[it.row, 0, hop], x_recv.at[it.row, 0, hop], right)

    def go_left(it, hop):
        mine = column(it, x, core) if hop == 0 else column(it, x_right, core, LINE // 2, LINE // 2)
        return put(mine, mine, x_send.at[it.row, 1, hop], x_recv.at[it.row, 1, hop], left)

    def go_across(it, k):
        mine = column(it, (x, x_left, x_right, x_far)[k], core)
        return put(mine, mine, s_send.at[it.row, k], s_recv.at[it.row, k], sibling)

    def await_up(it, hop):
        got = block(it, d - hop)
        put(got, got, z_send.at[it.row, 0, hop - 1], z_recv.at[it.row, 0, hop - 1], up).wait_recv()

    def await_down(it, hop):
        got = block(it, d + hop)
        put(got, got, z_send.at[it.row, 1, hop - 1], z_recv.at[it.row, 1, hop - 1], down).wait_recv()

    def await_right(it, hop):
        got = column(it, x_left, core) if hop == 0 else column(it, x_far, core, 0, LINE // 2)
        put(got, got, x_send.at[it.row, 0, hop], x_recv.at[it.row, 0, hop], right).wait_recv()

    def await_left(it, hop):
        got = column(it, x_right, core) if hop == 0 else column(it, x_far, core, LINE // 2, LINE // 2)
        put(got, got, x_send.at[it.row, 1, hop], x_recv.at[it.row, 1, hop], left).wait_recv()

    def await_across(it, k):
        got = column(it, (x, x_left, x_right, x_far)[k], 1 - core)
        put(got, got, s_send.at[it.row, k], s_recv.at[it.row, k], sibling).wait_recv()

    def direct_up(it, k):
        mine = block(it, d)
        return put(mine, mine, z_send.at[it.row, 0, k - 1], z_recv.at[it.row, 0, k - 1], {"expert": e + 2 * away * k})

    def direct_down(it, k):
        mine = block(it, d)
        return put(mine, mine, z_send.at[it.row, 1, k - 1], z_recv.at[it.row, 1, k - 1], {"expert": e - 2 * away * k})

    def direct(it, what):
        for k in range(1, LINE):

            @pl.when(d + k < LINE)
            def _():
                what(direct_up(it, k))

            @pl.when(d >= k)
            def _():
                what(direct_down(it, k))

    def stage0_direct(it):
        direct(it, lambda copy: copy.start())

    def stage0(it):
        @pl.when(d < LINE - 1)
        def _():
            go_up(it, 0).start()

        @pl.when(d > 1)
        def _():
            go_down(it, 0).start()

    def along_line(it, hop):
        @pl.when(d >= hop)
        def _():
            await_up(it, hop)
            if hop < LINE - 1:

                @pl.when(d < LINE - 1)
                def _():
                    go_up(it, hop).start()

        @pl.when((d >= 1) & (d < LINE - hop))
        def _():
            await_down(it, hop)
            if hop < LINE - 1:

                @pl.when(d > 1)
                def _():
                    go_down(it, hop).start()

    def await_line(it):
        for hop in range(1, LINE):

            @pl.when(d >= hop)
            def _():
                await_up(it, hop)

            @pl.when(d < LINE - hop)
            def _():
                await_down(it, hop)

    def along_ring(it):
        go_right(it, 0).start()
        go_left(it, 0).start()
        go_across(it, 0).start()

    def stage4(it):
        await_right(it, 0)
        go_right(it, 1).start()
        go_across(it, 1).start()
        await_left(it, 0)
        go_left(it, 1).start()
        go_across(it, 2).start()

    def stage5(it):
        await_right(it, 1)
        await_left(it, 1)
        go_across(it, 3).start()

    def stage6(it):
        for k in range(4):
            await_across(it, k)

    def sent_line(it):
        for hop in range(LINE - 1):

            @pl.when((d >= hop) & (d < LINE - 1))
            def _():
                go_up(it, hop).wait_send()

            @pl.when((d < LINE - hop) & (d > 1))
            def _():
                go_down(it, hop).wait_send()

    def sent(it):
        for hop in range(2):
            go_right(it, hop).wait_send()
            go_left(it, hop).wait_send()
        for k in range(4):
            go_across(it, k).wait_send()

    def exchange(it):
        part = pl.ds(it.chunk, it.count)
        return put(own.at[part], back.at[part], e_send.at[it.row], e_recv.at[it.row], mirror)

    def hand_over(it):
        part = pl.ds(it.chunk, it.count)
        return put(own_near.at[part], own.at[part], n_send.at[it.row], n_recv.at[it.row], down)

    def lend():
        return put(hidden_out, hidden_in, h_send.at[0], h_recv.at[0], up)

    def make_hidden(part, parts):
        count = capacity // parts
        for k in range(count):
            c = part * count + k
            gate = pre[c, :, :width].astype(jnp.float32)
            lift = pre[c, :, width:].astype(jnp.float32)
            value = gate / (1.0 + jnp.exp(-gate)) * lift
            for half in range(width // 128):
                lanes = slice(half * 128, half * 128 + 128)
                at = pl.ds(pl.multiple_of(c * sources, sources), sources)
                hidden[half, at, :] = value[:, lanes]
                hidden_out[half, at, :] = value[:, lanes].astype(jnp.bfloat16)

    def turn_hidden(part, parts):
        count = sources // parts
        for k in range(count):
            s = part * count + k
            for half in range(width // 128):
                picked = hidden[half, pl.ds(s, capacity, stride=sources), :]
                turned[s, half * 128 : half * 128 + 128] = picked.T.astype(jnp.bfloat16)

    def spread_column(xx, of, spread=spread, expert=e):
        slot_of = lax.broadcasted_iota(jnp.int32, (capacity, tables.shape[2]), 0).astype(jnp.float32)
        first = (expert * 64).astype(jnp.float32)
        for zz in range(LINE):
            b = of * HALF + xx * LINE + zz
            code = tables[b, :TOP] - first
            named = (code >= 0.0) & (code < 64.0)
            slot = jnp.sum(jnp.where(named, code + 1.0, 0.0), axis=0, keepdims=True) - 1.0
            weight = jnp.sum(jnp.where(named, tables[b, TOP:], 0.0), axis=0, keepdims=True)
            onehot = (slot_of == slot).astype(jnp.bfloat16)
            picked = jnp.dot(
                turned[xx * (2 * LINE) + zz * 2 + of], onehot, preferred_element_type=jnp.float32
            )
            lanes = pl.ds(pl.multiple_of(b * 128, 128), 128)
            spread[:, lanes] = (picked * weight).astype(jnp.bfloat16)

    def product(it, spread, own):
        total = None
        step = 4
        for k in range(0, sources, step):
            parts = [rows[it.chunk + c, k : k + step].reshape(step * 128, COLS) for c in range(it.count)]
            part = parts[0] if it.count == 1 else jnp.concatenate(parts, axis=1)
            term = jnp.dot(spread[:, k * 128 : (k + step) * 128], part, preferred_element_type=jnp.float32)
            total = term if total is None else total + term
        for c in range(it.count):
            own[it.chunk + c] = total[:, c * COLS : (c + 1) * COLS].astype(jnp.bfloat16)

    def store(it):
        lanes = pl.ds(pl.multiple_of(it.chunk * COLS, COLS), it.count * COLS)
        return pltpu.make_async_copy(total_buf.at[:, lanes], out_ref.at[:, lanes], out_sem.at[it.row])

    def finish(it):
        exchange(it).wait_recv()
        exchange(it).wait_send()
        if it.count == 2:

            @pl.when(d == 1)
            def _():
                hand_over(it).wait_send()

        for c in range(it.count):
            j = it.chunk + c
            both = own[j].astype(jnp.float32) + back[j].astype(jnp.float32)
            total_buf[:, pl.ds(pl.multiple_of(j * COLS, COLS), COLS)] = both.astype(jnp.bfloat16)
        store(it).start()

    def relay(it):
        hand_over(it).wait_recv()
        exchange(it).start()

    def multiply_near(it):
        product(it, spread_near, own_near)
        hand_over(it).start()

    def multiply(it):
        stage6(it)
        product(it, spread, own)
        exchange(it).start()

    def multiply_two(it):
        stage6(it)

        @pl.when(d == 1)
        def _():
            multiply_near(it)

        product(it, spread, own)
        exchange(it).start()

    def loaded(it):
        for c in range(it.count):
            load(it.chunk + c).wait()

    @pl.loop(0, pairs + TWO["product"] + RECV_LAG)
    def _(i):
        gathers = d >= 1
        always = d >= 0

        def at_step(who, step, what, *args):
            @pl.when((i == step) & who)
            def _():
                what(*args)

        def of_pair(who, step, what, *args):
            @pl.when((i >= step) & (i < step + pairs) & who)
            def _():
                what(pair(i - step), *args)

        def ring_of(it):
            await_line(it)
            along_ring(it)

        def start_single(it):
            loaded(it)
            stage0_direct(it)

        def start_pair(it):
            loaded(it)
            stage0(it)

        def last_hop(it):
            along_line(it, 3)
            along_ring(it)

        def hide():
            pre_load.wait()
            pl.loop(0, 9)(lambda part: make_hidden(part, 9))

        def turn():
            pl.loop(0, 8)(lambda part: turn_hidden(part, 8))

        def spread_some(waits, columns):
            for k in waits:
                await_across(table, k)
            for column_of in columns:
                spread_column(*column_of)

        def borrow():
            lend().wait_recv()
            for half in range(width // 128):
                hidden[half] = hidden_in[half].astype(jnp.float32)
            turn()

            @pl.loop(0, RING)
            def _(k):
                spread_column(k, core, spread_near, near_e)
                spread_column(k, 1 - core, spread_near, near_e)

        def done_line(it):
            direct(it, lambda copy: copy.wait_send())

        of_pair(gathers, TWO["product"], multiply_two)

        at_step(always, 0, stage0_direct, table)
        at_step(always, 1, ring_of, table)
        at_step(always, 2, stage4, table)
        at_step(always, 3, stage5, table)
        for k in range(SINGLES):
            at_step(always, ONE["start"][k], start_single, single(k))
        for k in range(SINGLES):
            at_step(always, k + ONE["pass"], stage4, single(k))
        for k in range(SINGLES):
            at_step(always, k + ONE["ring"], ring_of, single(k))
        for k in range(SINGLES):
            at_step(always, k + ONE["far"], stage5, single(k))

        of_pair(gathers, TWO["far"], stage5)
        of_pair(gathers, TWO["pass"], stage4)
        of_pair(gathers, TWO["ring"], last_hop)
        of_pair(gathers, TWO["hop2"], along_line, 2)
        of_pair(gathers, TWO["hop1"], along_line, 1)
        of_pair(always, TWO["start"], start_pair)

        at_step(always, 1, hide)
        at_step(d == 0, 1, lambda: lend().start())
        at_step(always, 2, turn)
        at_step(always, 3, spread_some, (), ((x, core),))
        at_step(always, 3, spread_some, (0,), ((x, 1 - core), (x_left, core), (x_right, core)))
        rest = ((x_left, 1 - core), (x_right, 1 - core), (x_far, core), (x_far, 1 - core))
        at_step(always, 4, spread_some, (1, 2, 3), rest)

        for k in range(SINGLES):
            at_step(always, k + ONE["product"], multiply, single(k))
        at_step(d == 1, BORROW, borrow)

        at_step(always, 6, done_line, table)
        at_step(always, 6, sent, table)
        at_step(d == 0, 6, lambda: lend().wait_send())
        for k in range(SINGLES):
            at_step(always, k + ONE["product"] + 1, done_line, single(k))
            at_step(always, k + ONE["product"] + 1, sent, single(k))
        of_pair(always, TWO["product"], sent_line)
        of_pair(gathers, TWO["product"], sent)
        of_pair(d == 0, TWO["product"] + 1, relay)
        for k in range(SINGLES):
            at_step(always, k + TWO["product"] + 1, finish, single(k))
        of_pair(always, TWO["product"] + RECV_LAG, finish)

    for k in range(SINGLES):
        store(single(k)).wait()

    @pl.loop(0, pairs)
    def _(j):
        store(pair(j)).wait()


def body(grad_out, expert_ids, slot_pos, gate_probs, saved_pre):
    grad_rows = grad_out[0]
    saved = saved_pre[0, :, 0].transpose(1, 0, 2)
    tokens, model = grad_rows.shape
    capacity, sources, both = saved.shape
    width = both // 2
    chunks = model // COLS
    items = SINGLES + (chunks - SINGLES) // 2
    semaphores = (
        [(items + 1, 2, 3)] * 2 + [(items + 1, 2, 2)] * 2 + [(items + 1, 4)] * 2 + [(items,)] * 2
        + [(items,), (items,), (1,), (1,), (chunks,), (1,), (3,), (items,)]
    )
    anywhere = pl.BlockSpec(memory_space=pl.ANY)
    result = pl.pallas_call(
        functools.partial(kernel, chunks, capacity),
        out_shape=jax.ShapeDtypeStruct((width, model), jnp.bfloat16),
        in_specs=[anywhere] * 5,
        out_specs=anywhere,
        scratch_shapes=[
            pltpu.VMEM((chunks, sources, tokens, COLS), jnp.bfloat16),
            pltpu.VMEM((sources, 16, tokens), jnp.float32),
            pltpu.VMEM((2, TOP, tokens), jnp.int32),
            pltpu.VMEM((TOP, tokens), jnp.float32),
            pltpu.VMEM((capacity, sources, both), jnp.bfloat16),
            pltpu.VMEM((width // 128, capacity * sources, 128), jnp.float32),
            pltpu.VMEM((width // 128, capacity * sources, 128), jnp.bfloat16),
            pltpu.VMEM((width // 128, capacity * sources, 128), jnp.bfloat16),
            pltpu.VMEM((sources, width, capacity), jnp.bfloat16),
            pltpu.VMEM((width, sources * tokens), jnp.bfloat16),
            pltpu.VMEM((width, sources * tokens), jnp.bfloat16),
            pltpu.VMEM((chunks, width, COLS), jnp.bfloat16),
            pltpu.VMEM((chunks, width, COLS), jnp.bfloat16),
            pltpu.VMEM((chunks, width, COLS), jnp.bfloat16),
            pltpu.VMEM((width, model), jnp.bfloat16),
            *[pltpu.SemaphoreType.DMA(shape) for shape in semaphores],
        ],
        compiler_params=pltpu.CompilerParams(
            collective_id=0, has_side_effects=True, vmem_limit_bytes=62 * 1024 * 1024
        ),
        cost_estimate=pl.CostEstimate(
            flops=2 * sources * tokens * width * model,
            bytes_accessed=8 * 1024 * 1024,
            transcendentals=sources * capacity * width,
        ),
    )(expert_ids[0].T, slot_pos[0].T, gate_probs[0].T, grad_rows, saved)
    return result[None, None]


def solution(mesh):
    return jax.shard_map(
        body,
        mesh=mesh,
        in_specs=(
            P("pipe", "expert", None),
            P("pipe", "expert", None),
            P("pipe", "expert", None),
            P("pipe", "expert", None),
            P("pipe", None, "expert", None, None),
        ),
        out_specs=P("pipe", "expert", None, None),
        check_vma=False,
    )
```
